512 devices in a mesh: req: 64 (over z, x, core), tp: 8 (over y).
Axes of the slice: x: 4, y: 8, z: 8, core: 2. Of those that a mesh axis runs over, the one named last changes fastest.
Arguments:
- normed_hidden_input: bfloat16 [1024, 2, 8192], P('req', None, 'tp'), may hold values from -6 to 6
- value_matrix: bfloat16 [8192, 1024], P(None, 'tp'), may hold values from -0.0625 to 0.0625
- adapter_down_weight: bfloat16 [8192, 32768], P('tp', 'req'), may hold values from -0.0625 to 0.0625
- adapter_up_weight: bfloat16 [32768, 1024], P('req', 'tp'), may hold values from -0.75 to 0.75
- request_adapter: int32 [1024], P('req'), may hold values from 0 to 511, as said below
- adapter_storage_row: int32 [512], replicated, may hold values from 0 to 511, as said below
- cache_valid_length: int32 [1024], P('req'), may hold values from 2 to 64
- queries: bfloat16 [1024, 2, 8192], P('req', None, 'tp'), may hold values from -9 to 9
- stored_key_cache: bfloat16 [1024, 64, 1024], P('req', None, 'tp'), may hold values from -4 to 4
- stored_value_cache: bfloat16 [1024, 64, 1024], P('req', None, 'tp'), may hold values from -6 to 6
- step_keys: bfloat16 [1024, 2, 1024], P('req', None, 'tp'), may hold values from -6 to 6
Outputs:
- step_values: bfloat16 [1024, 2, 1024], P('req', None, 'tp')
- attention: bfloat16 [1024, 2, 8192], P('req', None, 'tp')
The draws below stay inside these ranges and needn't reach their ends.
Inputs may be any that keep to these rules, and one draw needn't show every extreme that they name: `request_adapter`: storage row p lies on home device p // 8. Of the 16 requests of one device, at most 2 use adapters stored on one home device; one home device gets exactly 2 from every device. `adapter_storage_row`: A permutation.
All inputs are finite; a program needn't handle non-finite values.
Results may differ from the reference program's by a relative error of at most 0.0053.
Values may be sent and summed in bfloat16 or wider, within the bound.
No kernel may reach another device: no remote copies, remote signals or barrier semaphores. Data moves between devices by JAX's collectives and lax.ppermute only.
A program may use at most 64 MiB of HBM per device.

```python
import math
import jax
import jax.numpy as jnp
from jax import lax

MODEL_WIDTH = 8192
QUERY_HEADS = 64
KEY_HEADS = 8
HEAD_WIDTH = 128
ADAPTER_RANK = 64
NEW_TOKENS = 2
CAP = 2
R_DEV = 16
ADAPT_DEV = 8
CACHE_SPAN = 64
QUERY_PER_KEY = 8
REQUEST_TOTAL = 1024
ADAPTER_TOTAL = 512


def adapter_tables(key):
    key = jax.random.fold_in(key, 11)
    key_perm, key_hot, key_flag, key_blocks, key_slot = jax.random.split(key, 5)
    homes_count = ADAPTER_TOTAL // ADAPT_DEV
    blocks = REQUEST_TOTAL // R_DEV
    storage_of = jax.random.permutation(key_perm, ADAPTER_TOTAL).astype(jnp.int32)
    owner_of = jnp.argsort(storage_of).astype(jnp.int32)
    hot_home = jax.random.randint(key_hot, (), 0, homes_count).astype(jnp.int32)
    if R_DEV + 1 <= homes_count:
        flags = jax.random.randint(key_flag, (blocks,), 0, 4) == 0
    else:
        flags = jnp.zeros((blocks,), dtype=bool)
    base_index = jnp.arange(R_DEV - CAP, dtype=jnp.int32)

    def block_homes(block_key, flagged):
        key_order, key_mix = jax.random.split(block_key)
        others = (hot_home + 1 + jax.random.permutation(key_order, homes_count - 1).astype(jnp.int32)) % homes_count
        repeated = jnp.tile(others, CAP)
        picks = jnp.where(flagged, jnp.maximum(base_index - 1, 0), base_index)
        listed = jnp.concatenate([jnp.full((CAP,), hot_home, dtype=jnp.int32), repeated[picks]])
        return listed[jax.random.permutation(key_mix, R_DEV)]
    homes = jax.vmap(block_homes)(jax.random.split(key_blocks, blocks), flags).reshape(-1)
    slots = jax.random.randint(key_slot, (REQUEST_TOTAL,), 0, ADAPT_DEV).astype(jnp.int32)
    return (storage_of, owner_of[homes * ADAPT_DEV + slots].astype(jnp.int32))


def draw_adapter_storage_row(key, part):
    return adapter_tables(key)[0]


def draw_request_adapter(key, part):
    return adapter_tables(key)[1]


def draw_cache_valid_length(key, part):
    key = jax.random.fold_in(key, 23)
    key_len, key_spot = jax.random.split(key)
    lengths = jax.random.randint(key_len, (REQUEST_TOTAL,), 2, CACHE_SPAN + 1).astype(jnp.int32)
    spot = jax.random.randint(key_spot, (), 0, REQUEST_TOTAL)
    return jnp.where(jnp.arange(REQUEST_TOTAL) == spot, CACHE_SPAN, lengths).astype(jnp.int32)


def attention_tables(key):
    key = jax.random.fold_in(key, 37)
    key_q, random_key_seed = jax.random.split(key, 2)
    query_all = jnp.clip(jax.random.normal(key_q, (REQUEST_TOTAL, NEW_TOKENS, QUERY_HEADS * HEAD_WIDTH), jnp.float32), -4.0, 4.0)
    joined_keys = jnp.clip(jax.random.normal(random_key_seed, (REQUEST_TOTAL, CACHE_SPAN, KEY_HEADS * HEAD_WIDTH), jnp.float32), -4.0, 4.0)
    return (query_all, joined_keys)


def draw_queries(key, part):
    return attention_tables(key)[0].astype(jnp.bfloat16)


def draw_stored_key_cache(key, part):
    return attention_tables(key)[1].astype(jnp.bfloat16)


def steps_of(stream_key, dims, cuts, smallest, largest):
    def one(position, shards_of):
        draws = jax.random.uniform(jax.random.fold_in(jax.random.fold_in(stream_key, 6), position), (shards_of,), jnp.float32, smallest / len(cuts), largest / len(cuts))
        return jnp.repeat(jnp.exp(draws), dims[position] // shards_of).reshape((-1,) + (1,) * (len(dims) - position - 1))

    gain = one(*cuts[0])
    for cut in cuts[1:]:
        gain = gain * one(*cut)
    return gain


def bell_draw(own_key, extent, width, reach, pieces=(), kind=jnp.bfloat16):
    level = steps_of(own_key, extent, pieces, -0.22, 0.18) if pieces else 1.0
    entries = jax.random.normal(own_key, extent, jnp.float32) * width * level
    return jnp.minimum(jnp.maximum(entries, -reach), reach).astype(kind)


def setup_inputs(seed: int = 0) -> dict:
    streams_of = jax.random.split(jax.random.key(seed), 12)
    normed_hidden_input = bell_draw(streams_of[0], (REQUEST_TOTAL, NEW_TOKENS, MODEL_WIDTH), 1.0, 6.0, ((0, 64), (2, 8)))
    value_matrix = bell_draw(streams_of[1], (MODEL_WIDTH, KEY_HEADS * HEAD_WIDTH), MODEL_WIDTH ** -0.5, 0.0625, ((1, 8),))
    adapter_down_weight = bell_draw(streams_of[2], (MODEL_WIDTH, ADAPTER_TOTAL * ADAPTER_RANK), MODEL_WIDTH ** -0.5, 0.0625, ((0, 8), (1, 64)))
    adapter_up_weight = bell_draw(streams_of[3], (ADAPTER_TOTAL * ADAPTER_RANK, KEY_HEADS * HEAD_WIDTH), ADAPTER_RANK ** -0.5, 0.75, ((0, 64), (1, 8)))
    request_adapter = draw_request_adapter(jax.random.fold_in(streams_of[11], 71), 0)
    adapter_storage_row = draw_adapter_storage_row(jax.random.fold_in(streams_of[11], 71), 0)
    cache_valid_length = draw_cache_valid_length(jax.random.fold_in(streams_of[11], 71), 0)
    queries = draw_queries(jax.random.fold_in(streams_of[11], 71), 0)
    stored_key_cache = draw_stored_key_cache(jax.random.fold_in(streams_of[11], 71), 0)
    stored_value_cache = bell_draw(streams_of[9], (REQUEST_TOTAL, CACHE_SPAN, KEY_HEADS * HEAD_WIDTH), 1.0, 6.0, ((0, 64), (2, 8)))
    step_keys = bell_draw(streams_of[10], (REQUEST_TOTAL, NEW_TOKENS, KEY_HEADS * HEAD_WIDTH), 1.0, 6.0, ((0, 64), (2, 8)))
    return {"normed_hidden_input": normed_hidden_input, "value_matrix": value_matrix, "adapter_down_weight": adapter_down_weight, "adapter_up_weight": adapter_up_weight, "request_adapter": request_adapter, "adapter_storage_row": adapter_storage_row, "cache_valid_length": cache_valid_length, "queries": queries, "stored_key_cache": stored_key_cache, "stored_value_cache": stored_value_cache, "step_keys": step_keys}


def reference(normed_hidden_input, value_matrix, adapter_down_weight, adapter_up_weight, request_adapter, adapter_storage_row, cache_valid_length, queries, stored_key_cache, stored_value_cache, step_keys):
    storage = adapter_storage_row[request_adapter].astype(jnp.int32)
    flattened_rows = normed_hidden_input.reshape(REQUEST_TOTAL * NEW_TOKENS, MODEL_WIDTH)
    plain_values = jnp.dot(flattened_rows, value_matrix, preferred_element_type=jnp.float32).reshape(REQUEST_TOTAL, NEW_TOKENS, KEY_HEADS * HEAD_WIDTH)
    picked_down_weight = adapter_down_weight.reshape(MODEL_WIDTH, ADAPTER_TOTAL, ADAPTER_RANK)
    picked_up_weight = adapter_up_weight.reshape(ADAPTER_TOTAL, ADAPTER_RANK, KEY_HEADS * HEAD_WIDTH)

    def one_request(packed):
        request_rows, where_stored = packed
        down_one = lax.dynamic_index_in_dim(picked_down_weight, where_stored, 1, keepdims=False)
        up_one = lax.dynamic_index_in_dim(picked_up_weight, where_stored, 0, keepdims=False)
        reduced = jnp.dot(request_rows, down_one, preferred_element_type=jnp.float32).astype(jnp.bfloat16)
        return jnp.dot(reduced, up_one, preferred_element_type=jnp.float32).astype(jnp.bfloat16)
    lowrank = lax.map(one_request, (normed_hidden_input, storage))
    step_values = (plain_values + lowrank.astype(jnp.float32)).astype(jnp.bfloat16)
    scale = 1.0 / math.sqrt(HEAD_WIDTH)
    query_head_view = queries.reshape(REQUEST_TOTAL, NEW_TOKENS, KEY_HEADS, QUERY_PER_KEY, HEAD_WIDTH).astype(jnp.float32)
    key_head_view = stored_key_cache.reshape(REQUEST_TOTAL, CACHE_SPAN, KEY_HEADS, HEAD_WIDTH).astype(jnp.float32)
    current_keys = step_keys.reshape(REQUEST_TOTAL, NEW_TOKENS, KEY_HEADS, HEAD_WIDTH).astype(jnp.float32)
    cache_scores = jnp.einsum('rskgd,rckd->rskgc', query_head_view, key_head_view) * scale
    fresh_scores = jnp.einsum('rskgd,rtkd->rskgt', query_head_view, current_keys) * scale
    valid = jnp.arange(CACHE_SPAN, dtype=jnp.int32)[None, :] < cache_valid_length[:, None]
    causal = jnp.arange(NEW_TOKENS, dtype=jnp.int32)[None, :] <= jnp.arange(NEW_TOKENS, dtype=jnp.int32)[:, None]
    cache_scores = jnp.where(valid[:, None, None, None, :], cache_scores, -jnp.inf)
    fresh_scores = jnp.where(causal[None, :, None, None, :], fresh_scores, -jnp.inf)
    scores = jnp.concatenate([cache_scores, fresh_scores], axis=-1)
    peak = lax.optimization_barrier(jnp.max(scores, axis=-1, keepdims=True))
    expo = jnp.exp(scores - peak)
    weights = (expo / lax.optimization_barrier(jnp.sum(expo, axis=-1, keepdims=True))).astype(jnp.bfloat16)
    joined_values = jnp.concatenate([stored_value_cache.reshape(REQUEST_TOTAL, CACHE_SPAN, KEY_HEADS, HEAD_WIDTH), step_values.reshape(REQUEST_TOTAL, NEW_TOKENS, KEY_HEADS, HEAD_WIDTH)], axis=1)
    attended = jnp.einsum('rskgc,rckd->rskgd', weights.astype(jnp.float32), joined_values.astype(jnp.float32))
    attention = attended.astype(jnp.bfloat16).reshape(REQUEST_TOTAL, NEW_TOKENS, QUERY_HEADS * HEAD_WIDTH)
    return (step_values, attention)
```

```python
import math

import jax
import jax.numpy as jnp
from jax import lax
from jax.sharding import PartitionSpec as P

HEAD_WIDTH = 128
ADAPTER_RANK = 64
QUERY_PER_KEY = 8
CAP = 2
BF = jnp.bfloat16
F32 = jnp.float32


def body(
    normed_hidden_input,
    value_matrix,
    adapter_down_weight,
    adapter_up_weight,
    request_adapter,
    adapter_storage_row,
    cache_valid_length,
    queries,
    stored_key_cache,
    stored_value_cache,
    step_keys,
):
    x = normed_hidden_input
    R, S, W = x.shape
    V = value_matrix.shape[1]
    A = adapter_up_weight.shape[0] // ADAPTER_RANK
    H = lax.axis_size("req")
    T = lax.axis_size("tp")
    total_adapters = adapter_storage_row.shape[0]
    matches = request_adapter[:, None] == jnp.arange(total_adapters, dtype=jnp.int32)[None, :]
    storage = jnp.sum(jnp.where(matches, adapter_storage_row[None, :], 0), axis=1)
    home = storage // A
    slot = storage % A
    same = (home[:, None] == home[None, :]) & (jnp.arange(R)[None, :] < jnp.arange(R)[:, None])
    place = home * CAP + jnp.sum(same.astype(jnp.int32), axis=1)
    pick = (place[None, :] == jnp.arange(H * CAP, dtype=jnp.int32)[:, None]).astype(BF)
    code = jnp.broadcast_to(slot.astype(BF)[:, None, None], (R, S, 128))
    outgoing = jnp.einsum(
        "ki,isd->ksd", pick, jnp.concatenate([x, code], axis=2), preferred_element_type=F32
    ).astype(BF)
    arrived = lax.all_to_all(outgoing.reshape(H, CAP * S, W + 128), "req", 0, 0)
    arrived = arrived.reshape(H * CAP * S, W + 128)
    rows = H * CAP * S
    row_slot = arrived[:, W].astype(jnp.int32)
    projected = jnp.dot(arrived[:, :W], adapter_down_weight, preferred_element_type=F32)
    chosen = row_slot[:, None] == jnp.arange(A, dtype=jnp.int32)[None, :]
    partial = jnp.sum(
        jnp.where(chosen[:, :, None], projected.reshape(rows, A, ADAPTER_RANK), 0.0), axis=1
    )
    partial = jnp.concatenate([partial[: rows // 2], partial[rows // 2 :]], axis=1)
    high = partial.astype(BF)
    low = (partial - high.astype(F32)).astype(BF)
    message = jnp.concatenate(
        [high, low] + [x[:, s, c * 128 : (c + 1) * 128] for s in range(S) for c in range(W // 128)],
        axis=0,
    )
    message = jnp.broadcast_to(message[None], (T,) + message.shape)
    message = lax.all_to_all(message, "tp", 0, 0)
    half = rows // 2
    summed = jnp.sum(
        message[:, :half].astype(F32) + message[:, half : 2 * half].astype(F32), axis=0
    ).astype(BF)
    summed = jnp.concatenate([summed[:, :ADAPTER_RANK], summed[:, ADAPTER_RANK:]], axis=0)
    spread = jnp.where(chosen[:, :, None], summed[:, None, :], jnp.zeros((), BF))
    back = jnp.dot(
        spread.reshape(rows, A * ADAPTER_RANK), adapter_up_weight, preferred_element_type=F32
    ).astype(BF)
    back = lax.all_to_all(back.reshape(H, CAP * S, V), "req", 0, 0)
    low_rank = jnp.einsum(
        "ki,ksd->isd", pick, back.reshape(H * CAP, S, V), preferred_element_type=F32
    ).reshape(R, S, V)
    full = message[:, 2 * half :].reshape(T, S, W // 128, R, 128)
    base = jnp.einsum(
        "tscrl,tclv->rsv",
        full,
        value_matrix.reshape(T, W // 128, 128, V),
        preferred_element_type=F32,
    )
    step_values = (base + low_rank).astype(BF)

    kv_local = V // HEAD_WIDTH
    scale = 1.0 / math.sqrt(HEAD_WIDTH)
    query_head_view = queries.reshape(R, S, kv_local, QUERY_PER_KEY, HEAD_WIDTH)
    key_head_view = stored_key_cache.reshape(R, -1, kv_local, HEAD_WIDTH)
    value_view = stored_value_cache.reshape(R, -1, kv_local, HEAD_WIDTH)
    current_keys = step_keys.reshape(R, S, kv_local, HEAD_WIDTH)
    fresh_values = step_values.reshape(R, S, kv_local, HEAD_WIDTH)
    context = key_head_view.shape[1]
    cache_scores = (
        jnp.einsum("rskgd,rckd->rskgc", query_head_view, key_head_view, preferred_element_type=F32)
        * scale
    )
    fresh_scores = (
        jnp.einsum("rskgd,rtkd->rskgt", query_head_view, current_keys, preferred_element_type=F32)
        * scale
    )
    valid = jnp.arange(context, dtype=jnp.int32)[None, :] < cache_valid_length[:, None]
    causal = (
        jnp.arange(S, dtype=jnp.int32)[None, :] <= jnp.arange(S, dtype=jnp.int32)[:, None]
    )
    cache_scores = jnp.where(valid[:, None, None, None, :], cache_scores, -jnp.inf)
    fresh_scores = jnp.where(causal[None, :, None, None, :], fresh_scores, -jnp.inf)
    peak = jnp.maximum(jnp.max(cache_scores, axis=-1), jnp.max(fresh_scores, axis=-1))[..., None]
    cache_expo = jnp.exp(cache_scores - peak)
    fresh_expo = jnp.exp(fresh_scores - peak)
    denominator = jnp.sum(cache_expo, axis=-1, keepdims=True) + jnp.sum(
        fresh_expo, axis=-1, keepdims=True
    )
    cache_weights = (cache_expo / denominator).astype(BF)
    fresh_weights = (fresh_expo / denominator).astype(BF)
    attended = jnp.einsum(
        "rskgc,rckd->rskgd", cache_weights, value_view, preferred_element_type=F32
    )
    attended = attended + jnp.einsum(
        "rskgt,rtkd->rskgd", fresh_weights, fresh_values, preferred_element_type=F32
    )
    attention = attended.astype(BF).reshape(R, S, kv_local * QUERY_PER_KEY * HEAD_WIDTH)
    return (step_values, attention)


def solution(mesh):
    placed = (
        P("req", None, "tp"),
        P(None, "tp"),
        P("tp", "req"),
        P("req", "tp"),
        P("req"),
        P(),
        P("req"),
        P("req", None, "tp"),
        P("req", None, "tp"),
        P("req", None, "tp"),
        P("req", None, "tp"),
    )
    return jax.shard_map(
        body,
        mesh=mesh,
        in_specs=placed,
        out_specs=(P("req", None, "tp"), P("req", None, "tp")),
        check_vma=False,
    )
```

```python
import functools
import math

import jax
import jax.numpy as jnp
from jax import lax
from jax.experimental import pallas as pl
from jax.experimental.pallas import tpu as pltpu
from jax.sharding import PartitionSpec as P

HEAD_WIDTH = 128
ADAPTER_RANK = 64
QUERY_PER_KEY = 8
CAP = 2
LANES = 128
BF = jnp.bfloat16
F32 = jnp.float32
I32 = jnp.int32


def iota(shape, dim):
    return lax.broadcasted_iota(I32, shape, dim)


def dot(a, b):
    return jnp.dot(a, b, preferred_element_type=F32)


def picker(place_ref, rows, steps, requests):
    shape = (rows, requests * steps)
    column = iota((1, requests * steps), 1)
    target = jnp.zeros((1, requests * steps), I32)
    for i in range(requests):
        target = jnp.where(column // steps == i, place_ref[i] * steps + column % steps, target)
    return jnp.where(iota(shape, 0) == target, 1.0, 0.0).astype(BF)


def route_kernel(adapters, adapter_ref, storage_ref, x_ref, send_ref, wide_ref, place_ref):
    requests, steps, width = x_ref.shape
    homes = send_ref.shape[0]
    rows = homes * CAP * steps
    storage = [storage_ref[adapter_ref[i]] for i in range(requests)]
    home = [s // adapters for s in storage]
    code = jnp.zeros((requests * steps, LANES), I32)
    row = iota((requests * steps, LANES), 0)
    for i in range(requests):
        earlier = jnp.int32(0)
        for k in range(i):
            earlier = earlier + (home[k] == home[i]).astype(I32)
        place_ref[i] = home[i] * CAP + earlier
        code = jnp.where(row // steps == i, storage[i] % adapters, code)
    x = x_ref[...].reshape(requests * steps, width)
    wide_ref[...] = x.astype(F32)
    pick = picker(place_ref, rows, steps, requests)
    send = dot(pick, jnp.concatenate([x, code.astype(F32).astype(BF)], axis=1))
    send_ref[...] = send.astype(BF).reshape(send_ref.shape)


def down_kernel(halves, seen_ref, down_ref, part_ref, code_ref):
    homes, per, width = seen_ref.shape
    width = width - LANES
    seen = seen_ref[...].reshape(homes * per, width + LANES)
    code = seen[:, width:].astype(F32)
    code_ref[...] = code
    product = dot(seen[:, :width], down_ref[...])
    lane = iota(code.shape, 1)
    own = jnp.zeros(code.shape, F32)
    for m in range(product.shape[1] // LANES):
        here = (2 * m + lane // ADAPTER_RANK).astype(F32) == code
        own = jnp.where(here, product[:, m * LANES : (m + 1) * LANES], own)
    own = own + pltpu.roll(own, ADAPTER_RANK, 1)
    half = own.shape[0] // 2
    part = jnp.where(iota((half, LANES), 1) < ADAPTER_RANK, own[:half], own[half:])
    pieces = []
    for _ in range(halves):
        high = part.astype(BF)
        pieces.append(high)
        part = part - high.astype(F32)
    part = jnp.concatenate(pieces, axis=0)
    for t in range(part_ref.shape[0]):
        part_ref[t] = part


def up_kernel(halves, part_ref, code_ref, up_ref, back_ref):
    code = code_ref[...]
    half = code.shape[0] // 2
    total = jnp.zeros((half, LANES), F32)
    for t in range(part_ref.shape[0]):
        for k in range(halves):
            total = total + part_ref[t, k * half : (k + 1) * half].astype(F32)
    total = total.astype(BF).astype(F32)
    turned = pltpu.roll(total, ADAPTER_RANK, 1)
    left = iota((half, LANES), 1) < ADAPTER_RANK
    both = jnp.concatenate(
        [jnp.where(left, total, turned), jnp.where(left, turned, total)], axis=0
    )
    lane = iota(code.shape, 1)
    spread = []
    for m in range(up_ref.shape[0] // LANES):
        here = (2 * m + lane // ADAPTER_RANK).astype(F32) == code
        spread.append(jnp.where(here, both, 0.0).astype(BF))
    back = dot(jnp.concatenate(spread, axis=1), up_ref[...]).astype(BF)
    back_ref[...] = back.reshape(back_ref.shape)


def scores_kernel(length_ref, q_ref, key_ref, value_ref, fresh_ref, part_ref, weight_ref):
    requests, steps, width = q_ref.shape
    context = key_ref.shape[1]
    groups = width // HEAD_WIDTH
    n = requests * steps
    scale = 1.0 / math.sqrt(HEAD_WIDTH)
    q = q_ref[...].reshape(n, width)
    q = jnp.concatenate(
        [q[:, g * HEAD_WIDTH : (g + 1) * HEAD_WIDTH] for g in range(groups)], axis=0
    )
    keys = key_ref[...].reshape(requests * context, HEAD_WIDTH)
    values = value_ref[...].reshape(requests * context, HEAD_WIDTH)
    fresh = fresh_ref[...].reshape(n, HEAD_WIDTH)
    contract = (((1,), (1,)), ((), ()))
    cached = lax.dot_general(q, keys, contract, preferred_element_type=F32) * scale
    new = lax.dot_general(q, fresh, contract, preferred_element_type=F32) * scale
    column = iota((1, requests * context), 1)
    limit = jnp.zeros((1, requests * context), I32)
    for i in range(requests):
        limit = jnp.where(column // context == i, length_ref[i], limit)
    owner = jnp.where(column % context < limit, column // context, -1)
    row = iota((groups * n, 1), 0) % n
    cached = jnp.where(row // steps == owner, cached, -jnp.inf)
    other = iota((1, n), 1)
    new = jnp.where(
        (row // steps == other // steps) & (other % steps <= row % steps), new, -jnp.inf
    )
    peak = jnp.maximum(
        jnp.max(cached, axis=1, keepdims=True), jnp.max(new, axis=1, keepdims=True)
    )
    cached = jnp.exp(cached - peak)
    new = jnp.exp(new - peak)
    total = jnp.sum(cached, axis=1, keepdims=True) + jnp.sum(new, axis=1, keepdims=True)
    weight_ref[...] = (new / total).astype(BF)
    part_ref[...] = dot((cached / total).astype(BF), values)


def base_kernel(wide_ref, value_ref, base_ref):
    width = wide_ref.shape[2]
    total = jnp.zeros(base_ref.shape, F32)
    for t in range(wide_ref.shape[0]):
        total = total + dot(wide_ref[t].astype(BF), value_ref[t * width : (t + 1) * width, :])
    base_ref[...] = total


def finish_kernel(place_ref, back_ref, base_ref, part_ref, weight_ref, step_ref, out_ref):
    requests, steps, width = out_ref.shape
    homes, per, columns = back_ref.shape
    n = requests * steps
    pick = picker(place_ref, homes * per, steps, requests)
    back = back_ref[...].reshape(homes * per, columns)
    low = lax.dot_general(pick, back, (((0,), (0,)), ((), ())), preferred_element_type=F32)
    step = (base_ref[...] + low).astype(BF)
    step_ref[...] = step.reshape(step_ref.shape)
    attended = (part_ref[...] + dot(weight_ref[...], step)).astype(BF)
    attended = jnp.concatenate(
        [attended[g * n : (g + 1) * n] for g in range(width // HEAD_WIDTH)], axis=1
    )
    out_ref[...] = attended.reshape(out_ref.shape)


VM = pl.BlockSpec(memory_space=pltpu.VMEM)
SM = pl.BlockSpec(memory_space=pltpu.SMEM)


def call(kernel, ins, outs, args, flops=0, bytes_accessed=0):
    return pl.pallas_call(
        kernel,
        in_specs=list(ins),
        out_specs=tuple(s for s, _ in outs),
        out_shape=tuple(o for _, o in outs),
        compiler_params=pltpu.CompilerParams(vmem_limit_bytes=32 * 1024 * 1024),
        cost_estimate=pl.CostEstimate(
            flops=flops, bytes_accessed=bytes_accessed, transcendentals=0
        ),
    )(*args)


def body(
    normed_hidden_input,
    value_matrix,
    adapter_down_weight,
    adapter_up_weight,
    request_adapter,
    adapter_storage_row,
    cache_valid_length,
    queries,
    stored_key_cache,
    stored_value_cache,
    step_keys,
):
    x = normed_hidden_input
    R, S, W = x.shape
    V = value_matrix.shape[1]
    A = adapter_up_weight.shape[0] // ADAPTER_RANK
    H = lax.axis_size("req")
    T = lax.axis_size("tp")
    rows = H * CAP * S
    groups = queries.shape[2] // HEAD_WIDTH
    halves = HALVES
    shape = jax.ShapeDtypeStruct
    send, wide, place = call(
        functools.partial(route_kernel, A),
        (SM, SM, VM),
        (
            (VM, shape((H, CAP * S, W + LANES), BF)),
            (VM, shape((R * S, W), F32)),
            (SM, shape((R,), I32)),
        ),
        (request_adapter, adapter_storage_row, x),
    )
    seen = lax.all_to_all(send, "req", 0, 0)
    wide = lax.all_gather(wide, "tp", axis=0)
    attended, weights = call(
        scores_kernel,
        (SM, VM, VM, VM, VM),
        ((VM, shape((groups * R * S, HEAD_WIDTH), F32)), (VM, shape((groups * R * S, R * S), BF))),
        (cache_valid_length, queries, stored_key_cache, stored_value_cache, step_keys),
        flops=10**8,
        bytes_accessed=10**6,
    )
    part, code = call(
        functools.partial(down_kernel, halves),
        (VM, VM),
        ((VM, shape((T, halves * rows // 2, LANES), BF)), (VM, shape((rows, LANES), F32))),
        (seen, adapter_down_weight),
    )
    part = lax.all_to_all(part, "tp", 0, 0)
    part, attended, weights = lax.optimization_barrier((part, attended, weights))
    (back,) = call(
        functools.partial(up_kernel, halves),
        (VM, VM, VM),
        ((VM, shape((H, CAP * S, V), BF)),),
        (part, code, adapter_up_weight),
    )
    back = lax.all_to_all(back, "req", 0, 0)
    (base,) = call(
        base_kernel, (VM, VM), ((VM, shape((R * S, V), F32)),), (wide, value_matrix)
    )
    step_values, attention = call(
        finish_kernel,
        (SM, VM, VM, VM, VM),
        ((VM, shape((R, S, V), BF)), (VM, shape((R, S, groups * HEAD_WIDTH), BF))),
        (place, back, base, attended, weights),
    )
    return (step_values, attention)


HALVES = 2


def solution(mesh):
    placed = (
        P("req", None, "tp"),
        P(None, "tp"),
        P("tp", "req"),
        P("req", "tp"),
        P("req"),
        P(),
        P("req"),
        P("req", None, "tp"),
        P("req", None, "tp"),
        P("req", None, "tp"),
        P("req", None, "tp"),
    )
    return jax.shard_map(
        body,
        mesh=mesh,
        in_specs=placed,
        out_specs=(P("req", None, "tp"), P("req", None, "tp")),
        check_vma=False,
    )
```

```python
import functools
import math

import jax
import jax.numpy as jnp
from jax import lax
from jax.experimental import pallas as pl
from jax.experimental.pallas import tpu as pltpu
from jax.sharding import PartitionSpec as P

HEAD_WIDTH = 128
ADAPTER_RANK = 64
QUERY_PER_KEY = 8
CAP = 2
LANES = 128
BF = jnp.bfloat16
F32 = jnp.float32
I32 = jnp.int32


def iota(shape, dim):
    return lax.broadcasted_iota(I32, shape, dim)


def dot(a, b):
    return jnp.dot(a, b, preferred_element_type=F32)


def picker(place_ref, rows, steps, requests):
    shape = (rows, requests * steps)
    column = iota((1, requests * steps), 1)
    target = jnp.zeros((1, requests * steps), I32)
    for i in range(requests):
        target = jnp.where(column // steps == i, place_ref[i] * steps + column % steps, target)
    return jnp.where(iota(shape, 0) == target, 1.0, 0.0).astype(BF)


def route_kernel(
    adapters, adapter_hbm, storage_hbm, x_hbm, send_ref, place_ref, adapter_ref, storage_ref, x_ref, sems
):
    copies = [
        pltpu.make_async_copy(adapter_hbm, adapter_ref, sems.at[0]),
        pltpu.make_async_copy(storage_hbm, storage_ref, sems.at[1]),
        pltpu.make_async_copy(x_hbm, x_ref, sems.at[2]),
    ]
    for copy in copies:
        copy.start()
    requests, steps, width = x_ref.shape
    homes = send_ref.shape[0]
    rows = homes * CAP * steps
    copies[0].wait()
    copies[1].wait()
    storage = [storage_ref[adapter_ref[i]] for i in range(requests)]
    home = [s // adapters for s in storage]
    code = jnp.zeros((requests * steps, LANES), I32)
    row = iota((requests * steps, LANES), 0)
    for i in range(requests):
        earlier = jnp.int32(0)
        for k in range(i):
            earlier = earlier + (home[k] == home[i]).astype(I32)
        place_ref[i] = home[i] * CAP + earlier
        code = jnp.where(row // steps == i, storage[i] % adapters, code)
    pick = picker(place_ref, rows, steps, requests)
    copies[2].wait()
    x = x_ref[...].reshape(requests * steps, width)
    send = dot(pick, jnp.concatenate([x, code.astype(F32).astype(BF)], axis=1))
    send_ref[...] = send.astype(BF).reshape(send_ref.shape)


def down_kernel(halves, seen_ref, down_hbm, part_ref, code_hbm, down_ref, code_ref, sems):
    homes, per, width = seen_ref.shape
    width = width - LANES
    pieces = down_ref.shape[0]
    deep = width // pieces
    copies = [
        pltpu.make_async_copy(down_hbm.at[pl.ds(k * deep, deep)], down_ref.at[k], sems.at[k])
        for k in range(pieces)
    ]
    for copy in copies:
        copy.start()
    seen = seen_ref[...].reshape(homes * per, width + LANES)
    code = seen[:, width:].astype(F32)
    code_ref[...] = code
    save = pltpu.make_async_copy(code_ref, code_hbm, sems.at[pieces])
    save.start()
    product = jnp.zeros((homes * per, down_ref.shape[2]), F32)
    for k in range(pieces):
        copies[k].wait()
        product = product + dot(seen[:, k * deep : (k + 1) * deep], down_ref[k])
    lane = iota(code.shape, 1)
    own = jnp.zeros(code.shape, F32)
    for m in range(product.shape[1] // LANES):
        here = (2 * m + lane // ADAPTER_RANK).astype(F32) == code
        own = jnp.where(here, product[:, m * LANES : (m + 1) * LANES], own)
    own = own + pltpu.roll(own, ADAPTER_RANK, 1)
    half = own.shape[0] // 2
    part = jnp.where(iota((half, LANES), 1) < ADAPTER_RANK, own[:half], own[half:])
    pieces = []
    for _ in range(halves):
        high = part.astype(BF)
        pieces.append(high)
        part = part - high.astype(F32)
    part = jnp.concatenate(pieces, axis=0)
    for t in range(part_ref.shape[0]):
        part_ref[t] = part
    save.wait()


def up_kernel(halves, part_ref, code_hbm, up_hbm, back_ref, code_ref, up_ref, sems):
    copies = [
        pltpu.make_async_copy(code_hbm, code_ref, sems.at[0]),
        pltpu.make_async_copy(up_hbm, up_ref, sems.at[1]),
    ]
    for copy in copies:
        copy.start()
    half = code_ref.shape[0] // 2
    total = jnp.zeros((half, LANES), F32)
    for t in range(part_ref.shape[0]):
        for k in range(halves):
            total = total + part_ref[t, k * half : (k + 1) * half].astype(F32)
    total = total.astype(BF).astype(F32)
    turned = pltpu.roll(total, ADAPTER_RANK, 1)
    left = iota((half, LANES), 1) < ADAPTER_RANK
    both = jnp.concatenate(
        [jnp.where(left, total, turned), jnp.where(left, turned, total)], axis=0
    )
    copies[0].wait()
    code = code_ref[...]
    lane = iota(code.shape, 1)
    spread = []
    for m in range(up_ref.shape[0] // LANES):
        here = (2 * m + lane // ADAPTER_RANK).astype(F32) == code
        spread.append(jnp.where(here, both, 0.0).astype(BF))
    copies[1].wait()
    back = dot(jnp.concatenate(spread, axis=1), up_ref[...]).astype(BF)
    back_ref[...] = back.reshape(back_ref.shape)


def scores_kernel(length_ref, q_ref, key_ref, value_ref, fresh_ref, part_ref, weight_ref):
    requests, steps, width = q_ref.shape
    context = key_ref.shape[1]
    groups = width // HEAD_WIDTH
    n = requests * steps
    scale = 1.0 / math.sqrt(HEAD_WIDTH)
    q = q_ref[...].reshape(n, width)
    q = jnp.concatenate(
        [q[:, g * HEAD_WIDTH : (g + 1) * HEAD_WIDTH] for g in range(groups)], axis=0
    )
    keys = key_ref[...].reshape(requests * context, HEAD_WIDTH)
    values = value_ref[...].reshape(requests * context, HEAD_WIDTH)
    fresh = fresh_ref[...].reshape(n, HEAD_WIDTH)
    contract = (((1,), (1,)), ((), ()))
    cached = lax.dot_general(q, keys, contract, preferred_element_type=F32) * scale
    new = lax.dot_general(q, fresh, contract, preferred_element_type=F32) * scale
    column = iota((1, requests * context), 1)
    limit = jnp.zeros((1, requests * context), I32)
    for i in range(requests):
        limit = jnp.where(column // context == i, length_ref[i], limit)
    owner = jnp.where(column % context < limit, column // context, -1)
    row = iota((groups * n, 1), 0) % n
    cached = jnp.where(row // steps == owner, cached, -jnp.inf)
    other = iota((1, n), 1)
    new = jnp.where(
        (row // steps == other // steps) & (other % steps <= row % steps), new, -jnp.inf
    )
    peak = jnp.maximum(
        jnp.max(cached, axis=1, keepdims=True), jnp.max(new, axis=1, keepdims=True)
    )
    cached = jnp.exp(cached - peak)
    new = jnp.exp(new - peak)
    total = jnp.sum(cached, axis=1, keepdims=True) + jnp.sum(new, axis=1, keepdims=True)
    weight_ref[...] = (new / total).astype(BF)
    part_ref[...] = dot((cached / total).astype(BF), values)


def base_kernel(index_ref, x_ref, far_ref, *refs):
    value_ref, base_ref = refs[-2:]
    requests, steps, width = x_ref.shape
    rows = requests * steps
    mine = index_ref[0]
    pieces = [(0, x_ref[...]), (4, far_ref[...])]
    for k, ref in enumerate(refs[:-2]):
        pieces.append((k + 1, ref[:requests]))
        pieces.append((k + 5, ref[requests:]))
    total = jnp.zeros(base_ref.shape, F32)
    for other, piece in pieces:
        start = pl.multiple_of((mine ^ other) * width, width)
        total = total + dot(piece.reshape(rows, width), value_ref[pl.ds(start, width), :])
    base_ref[...] = total


def finish_kernel(place_ref, back_ref, base_ref, part_ref, weight_ref, step_ref, out_ref):
    requests, steps, width = out_ref.shape
    homes, per, columns = back_ref.shape
    n = requests * steps
    pick = picker(place_ref, homes * per, steps, requests)
    back = back_ref[...].reshape(homes * per, columns)
    low = lax.dot_general(pick, back, (((0,), (0,)), ((), ())), preferred_element_type=F32)
    step = (base_ref[...] + low).astype(BF)
    step_ref[...] = step.reshape(step_ref.shape)
    attended = (part_ref[...] + dot(weight_ref[...], step)).astype(BF)
    attended = jnp.concatenate(
        [attended[g * n : (g + 1) * n] for g in range(width // HEAD_WIDTH)], axis=1
    )
    out_ref[...] = attended.reshape(out_ref.shape)


VM = pl.BlockSpec(memory_space=pltpu.VMEM)
SM = pl.BlockSpec(memory_space=pltpu.SMEM)
HB = pl.BlockSpec(memory_space=pltpu.HBM)


def call(kernel, ins, outs, args, scratch=(), flops=0, bytes_accessed=0, mib=16):
    return pl.pallas_call(
        kernel,
        in_specs=list(ins),
        out_specs=tuple(s for s, _ in outs),
        out_shape=tuple(o for _, o in outs),
        scratch_shapes=list(scratch),
        compiler_params=pltpu.CompilerParams(vmem_limit_bytes=mib * 1024 * 1024),
        cost_estimate=pl.CostEstimate(
            flops=flops, bytes_accessed=bytes_accessed, transcendentals=0
        ),
    )(*args)


def body(
    normed_hidden_input,
    value_matrix,
    adapter_down_weight,
    adapter_up_weight,
    request_adapter,
    adapter_storage_row,
    cache_valid_length,
    queries,
    stored_key_cache,
    stored_value_cache,
    step_keys,
):
    x = normed_hidden_input
    R, S, W = x.shape
    V = value_matrix.shape[1]
    A = adapter_up_weight.shape[0] // ADAPTER_RANK
    H = lax.axis_size("req")
    T = lax.axis_size("tp")
    rows = H * CAP * S
    groups = queries.shape[2] // HEAD_WIDTH
    halves = HALVES
    shape = jax.ShapeDtypeStruct
    send, place = call(
        functools.partial(route_kernel, A),
        (HB, HB, HB),
        ((VM, shape((H, CAP * S, W + LANES), BF)), (SM, shape((R,), I32))),
        (request_adapter, adapter_storage_row, x),
        (
            pltpu.SMEM(request_adapter.shape, I32),
            pltpu.SMEM(adapter_storage_row.shape, I32),
            pltpu.VMEM(x.shape, BF),
            pltpu.SemaphoreType.DMA((3,)),
        ),
        mib=60,
    )
    seen = lax.all_to_all(send, "req", 0, 0)
    x, send = lax.optimization_barrier((x, send))
    swap = lambda v, d: lax.ppermute(v, "tp", [(i, i ^ d) for i in range(T)])
    far = swap(x, 4)
    pair = jnp.concatenate([x, far], axis=0)
    pairs = [swap(pair, d) for d in (1, 2, 3)]
    seen, far, pairs = lax.optimization_barrier((seen, far, pairs))
    attended, weights = call(
        scores_kernel,
        (SM, VM, VM, VM, VM),
        ((VM, shape((groups * R * S, HEAD_WIDTH), F32)), (VM, shape((groups * R * S, R * S), BF))),
        (cache_valid_length, queries, stored_key_cache, stored_value_cache, step_keys),
        flops=10**8,
        bytes_accessed=10**6,
        mib=60,
    )
    pieces = 4
    part, code = call(
        functools.partial(down_kernel, halves),
        (VM, HB),
        ((VM, shape((T, halves * rows // 2, LANES), BF)), (HB, shape((rows, LANES), F32))),
        (seen, adapter_down_weight),
        (
            pltpu.VMEM((pieces, W // pieces, adapter_down_weight.shape[1]), BF),
            pltpu.VMEM((rows, LANES), F32),
            pltpu.SemaphoreType.DMA((pieces + 1,)),
        ),
    )
    part = lax.all_to_all(part, "tp", 0, 0)
    part, attended, weights = lax.optimization_barrier((part, attended, weights))
    (back,) = call(
        functools.partial(up_kernel, halves),
        (VM, HB, HB),
        ((VM, shape((H, CAP * S, V), BF)),),
        (part, code, adapter_up_weight),
        (
            pltpu.VMEM((rows, LANES), F32),
            pltpu.VMEM(adapter_up_weight.shape, BF),
            pltpu.SemaphoreType.DMA((2,)),
        ),
    )
    back = lax.all_to_all(back, "req", 0, 0)
    mine = lax.axis_index("tp").astype(I32).reshape(1)
    (base,) = call(
        base_kernel,
        (SM, VM, VM) + (VM,) * len(pairs) + (VM,),
        ((VM, shape((R * S, V), F32)),),
        (mine, x, far, *pairs, value_matrix),
        flops=10**8,
        mib=60,
    )
    step_values, attention = call(
        finish_kernel,
        (SM, VM, VM, VM, VM),
        ((VM, shape((R, S, V), BF)), (VM, shape((R, S, groups * HEAD_WIDTH), BF))),
        (place, back, base, attended, weights),
    )
    return (step_values, attention)


HALVES = 2


def solution(mesh):
    placed = (
        P("req", None, "tp"),
        P(None, "tp"),
        P("tp", "req"),
        P("req", "tp"),
        P("req"),
        P(),
        P("req"),
        P("req", None, "tp"),
        P("req", None, "tp"),
        P("req", None, "tp"),
        P("req", None, "tp"),
    )
    return jax.shard_map(
        body,
        mesh=mesh,
        in_specs=placed,
        out_specs=(P("req", None, "tp"), P("req", None, "tp")),
        check_vma=False,
    )
```

```python
import functools
import math

import jax
import jax.numpy as jnp
from jax import lax
from jax.experimental import pallas as pl
from jax.experimental.pallas import tpu as pltpu
from jax.sharding import PartitionSpec as P

HEAD_WIDTH = 128
ADAPTER_RANK = 64
QUERY_PER_KEY = 8
CAP = 2
LANES = 128
BF = jnp.bfloat16
F32 = jnp.float32
I32 = jnp.int32


def iota(shape, dim):
    return lax.broadcasted_iota(I32, shape, dim)


def dot(a, b):
    return jnp.dot(a, b, preferred_element_type=F32)


def picker(place_ref, rows, steps, requests):
    shape = (rows, requests * steps)
    column = iota((1, requests * steps), 1)
    target = jnp.zeros((1, requests * steps), I32)
    for i in range(requests):
        target = jnp.where(column // steps == i, place_ref[i] * steps + column % steps, target)
    return jnp.where(iota(shape, 0) == target, 1.0, 0.0).astype(BF)


def route_kernel(
    adapters, adapter_hbm, storage_hbm, x_hbm, send_ref, place_ref, adapter_ref, storage_ref, x_ref, sems
):
    copies = [
        pltpu.make_async_copy(adapter_hbm, adapter_ref, sems.at[0]),
        pltpu.make_async_copy(storage_hbm, storage_ref, sems.at[1]),
        pltpu.make_async_copy(x_hbm, x_ref, sems.at[2]),
    ]
    for copy in copies:
        copy.start()
    requests, steps, width = x_ref.shape
    homes = send_ref.shape[0]
    rows = homes * CAP * steps
    copies[0].wait()
    copies[1].wait()
    storage = [storage_ref[adapter_ref[i]] for i in range(requests)]
    home = [s // adapters for s in storage]
    code = jnp.zeros((requests * steps, LANES), I32)
    row = iota((requests * steps, LANES), 0)
    for i in range(requests):
        earlier = jnp.int32(0)
        for k in range(i):
            earlier = earlier + (home[k] == home[i]).astype(I32)
        place_ref[i] = home[i] * CAP + earlier
        code = jnp.where(row // steps == i, storage[i] % adapters, code)
    pick = picker(place_ref, rows, steps, requests)
    copies[2].wait()
    x = x_ref[...].reshape(requests * steps, width)
    send = dot(pick, jnp.concatenate([x, code.astype(F32).astype(BF)], axis=1))
    send_ref[...] = send.astype(BF).reshape(send_ref.shape)


def down_kernel(halves, seen_ref, down_hbm, part_ref, code_hbm, down_ref, code_ref, sems):
    homes, per, width = seen_ref.shape
    width = width - LANES
    pieces = down_ref.shape[0]
    deep = width // pieces
    copies = [
        pltpu.make_async_copy(down_hbm.at[pl.ds(k * deep, deep)], down_ref.at[k], sems.at[k])
        for k in range(pieces)
    ]
    for copy in copies:
        copy.start()
    seen = seen_ref[...].reshape(homes * per, width + LANES)
    code = seen[:, width:].astype(F32)
    code_ref[...] = code
    save = pltpu.make_async_copy(code_ref, code_hbm, sems.at[pieces])
    save.start()
    product = jnp.zeros((homes * per, down_ref.shape[2]), F32)
    for k in range(pieces):
        copies[k].wait()
        product = product + dot(seen[:, k * deep : (k + 1) * deep], down_ref[k])
    lane = iota(code.shape, 1)
    own = jnp.zeros(code.shape, F32)
    for m in range(product.shape[1] // LANES):
        here = (2 * m + lane // ADAPTER_RANK).astype(F32) == code
        own = jnp.where(here, product[:, m * LANES : (m + 1) * LANES], own)
    own = own + pltpu.roll(own, ADAPTER_RANK, 1)
    half = own.shape[0] // 2
    part = jnp.where(iota((half, LANES), 1) < ADAPTER_RANK, own[:half], own[half:])
    pieces = []
    for _ in range(halves):
        high = part.astype(BF)
        pieces.append(high)
        part = part - high.astype(F32)
    part = jnp.concatenate(pieces, axis=0)
    for t in range(part_ref.shape[0]):
        part_ref[t] = part
    save.wait()


def up_kernel(halves, part_ref, code_hbm, up_hbm, back_ref, code_ref, up_ref, sems):
    copies = [
        pltpu.make_async_copy(code_hbm, code_ref, sems.at[0]),
        pltpu.make_async_copy(up_hbm, up_ref, sems.at[1]),
    ]
    for copy in copies:
        copy.start()
    half = code_ref.shape[0] // 2
    total = jnp.zeros((half, LANES), F32)
    for t in range(part_ref.shape[0]):
        for k in range(halves):
            total = total + part_ref[t, k * half : (k + 1) * half].astype(F32)
    total = total.astype(BF).astype(F32)
    turned = pltpu.roll(total, ADAPTER_RANK, 1)
    left = iota((half, LANES), 1) < ADAPTER_RANK
    both = jnp.concatenate(
        [jnp.where(left, total, turned), jnp.where(left, turned, total)], axis=0
    )
    copies[0].wait()
    code = code_ref[...]
    lane = iota(code.shape, 1)
    spread = []
    for m in range(up_ref.shape[0] // LANES):
        here = (2 * m + lane // ADAPTER_RANK).astype(F32) == code
        spread.append(jnp.where(here, both, 0.0).astype(BF))
    copies[1].wait()
    back = dot(jnp.concatenate(spread, axis=1), up_ref[...]).astype(BF)
    back_ref[...] = back.reshape(back_ref.shape)


def scores_kernel(length_ref, q_ref, key_ref, value_ref, fresh_ref, part_ref, weight_ref):
    requests, steps, width = q_ref.shape
    context = key_ref.shape[1]
    groups = width // HEAD_WIDTH
    n = requests * steps
    scale = 1.0 / math.sqrt(HEAD_WIDTH)
    q = q_ref[...].reshape(n, width)
    q = jnp.concatenate(
        [q[:, g * HEAD_WIDTH : (g + 1) * HEAD_WIDTH] for g in range(groups)], axis=0
    )
    keys = key_ref[...].reshape(requests * context, HEAD_WIDTH)
    values = value_ref[...].reshape(requests * context, HEAD_WIDTH)
    fresh = fresh_ref[...].reshape(n, HEAD_WIDTH)
    contract = (((1,), (1,)), ((), ()))
    cached = lax.dot_general(q, keys, contract, preferred_element_type=F32) * scale
    new = lax.dot_general(q, fresh, contract, preferred_element_type=F32) * scale
    column = iota((1, requests * context), 1)
    limit = jnp.zeros((1, requests * context), I32)
    for i in range(requests):
        limit = jnp.where(column // context == i, length_ref[i], limit)
    owner = jnp.where(column % context < limit, column // context, -1)
    row = iota((groups * n, 1), 0) % n
    cached = jnp.where(row // steps == owner, cached, -jnp.inf)
    other = iota((1, n), 1)
    new = jnp.where(
        (row // steps == other // steps) & (other % steps <= row % steps), new, -jnp.inf
    )
    peak = jnp.maximum(
        jnp.max(cached, axis=1, keepdims=True), jnp.max(new, axis=1, keepdims=True)
    )
    cached = jnp.exp(cached - peak)
    new = jnp.exp(new - peak)
    total = jnp.sum(cached, axis=1, keepdims=True) + jnp.sum(new, axis=1, keepdims=True)
    weight_ref[...] = (new / total).astype(BF)
    part_ref[...] = dot((cached / total).astype(BF), values)


def base_kernel(index_ref, x_ref, far_ref, *refs):
    value_ref, base_ref = refs[-2:]
    requests, steps, width = x_ref.shape
    rows = requests * steps
    mine = index_ref[0]
    pieces = [(0, x_ref[...]), (4, far_ref[...])]
    for k, ref in enumerate(refs[:-2]):
        pieces.append((k + 1, ref[:requests]))
        pieces.append((k + 5, ref[requests:]))
    total = jnp.zeros(base_ref.shape, F32)
    for other, piece in pieces:
        start = pl.multiple_of((mine ^ other) * width, width)
        total = total + dot(piece.reshape(rows, width), value_ref[pl.ds(start, width), :])
    base_ref[...] = total


def finish_kernel(place_ref, back_ref, base_ref, part_ref, weight_ref, step_ref, out_ref):
    requests, steps, width = out_ref.shape
    homes, per, columns = back_ref.shape
    n = requests * steps
    pick = picker(place_ref, homes * per, steps, requests)
    back = back_ref[...].reshape(homes * per, columns)
    low = lax.dot_general(pick, back, (((0,), (0,)), ((), ())), preferred_element_type=F32)
    step = (base_ref[...] + low).astype(BF)
    step_ref[...] = step.reshape(step_ref.shape)
    attended = (part_ref[...] + dot(weight_ref[...], step)).astype(BF)
    attended = jnp.concatenate(
        [attended[g * n : (g + 1) * n] for g in range(width // HEAD_WIDTH)], axis=1
    )
    out_ref[...] = attended.reshape(out_ref.shape)


VM = pl.BlockSpec(memory_space=pltpu.VMEM)
SM = pl.BlockSpec(memory_space=pltpu.SMEM)
HB = pl.BlockSpec(memory_space=pltpu.HBM)


def call(kernel, ins, outs, args, scratch=(), flops=0, bytes_accessed=0, mib=16):
    return pl.pallas_call(
        kernel,
        in_specs=list(ins),
        out_specs=tuple(s for s, _ in outs),
        out_shape=tuple(o for _, o in outs),
        scratch_shapes=list(scratch),
        compiler_params=pltpu.CompilerParams(vmem_limit_bytes=mib * 1024 * 1024),
        cost_estimate=pl.CostEstimate(
            flops=flops, bytes_accessed=bytes_accessed, transcendentals=0
        ),
    )(*args)


def body(
    normed_hidden_input,
    value_matrix,
    adapter_down_weight,
    adapter_up_weight,
    request_adapter,
    adapter_storage_row,
    cache_valid_length,
    queries,
    stored_key_cache,
    stored_value_cache,
    step_keys,
):
    x = normed_hidden_input
    R, S, W = x.shape
    V = value_matrix.shape[1]
    A = adapter_up_weight.shape[0] // ADAPTER_RANK
    H = lax.axis_size("req")
    T = lax.axis_size("tp")
    rows = H * CAP * S
    groups = queries.shape[2] // HEAD_WIDTH
    halves = HALVES
    shape = jax.ShapeDtypeStruct
    send, place = call(
        functools.partial(route_kernel, A),
        (HB, HB, HB),
        ((VM, shape((H, CAP * S, W + LANES), BF)), (SM, shape((R,), I32))),
        (request_adapter, adapter_storage_row, x),
        (
            pltpu.SMEM(request_adapter.shape, I32),
            pltpu.SMEM(adapter_storage_row.shape, I32),
            pltpu.VMEM(x.shape, BF),
            pltpu.SemaphoreType.DMA((3,)),
        ),
        mib=60,
    )
    seen = lax.all_to_all(send, "req", 0, 0)
    x, send = lax.optimization_barrier((x, send))
    swap = lambda v, d: lax.ppermute(v, "tp", [(i, i ^ d) for i in range(T)])
    far = swap(x, 4)
    pair = jnp.concatenate([x, far], axis=0)
    pairs = [swap(pair, d) for d in (3,)]
    attended, weights = call(
        scores_kernel,
        (SM, VM, VM, VM, VM),
        ((VM, shape((groups * R * S, HEAD_WIDTH), F32)), (VM, shape((groups * R * S, R * S), BF))),
        (cache_valid_length, queries, stored_key_cache, stored_value_cache, step_keys),
        flops=10**8,
        bytes_accessed=10**6,
        mib=60,
    )
    seen, far, pair, pairs, attended, weights = lax.optimization_barrier(
        (seen, far, pair, pairs, attended, weights)
    )
    pieces = 4
    part, code = call(
        functools.partial(down_kernel, halves),
        (VM, HB),
        ((VM, shape((T, halves * rows // 2, LANES), BF)), (HB, shape((rows, LANES), F32))),
        (seen, adapter_down_weight),
        (
            pltpu.VMEM((pieces, W // pieces, adapter_down_weight.shape[1]), BF),
            pltpu.VMEM((rows, LANES), F32),
            pltpu.SemaphoreType.DMA((pieces + 1,)),
        ),
    )
    part, pair = lax.optimization_barrier((part, pair))
    near = [swap(pair, d) for d in (1, 2)]
    part = lax.all_to_all(part, "tp", 0, 0)
    part, near = lax.optimization_barrier((part, near))
    pairs = near + pairs
    (back,) = call(
        functools.partial(up_kernel, halves),
        (VM, HB, HB),
        ((VM, shape((H, CAP * S, V), BF)),),
        (part, code, adapter_up_weight),
        (
            pltpu.VMEM((rows, LANES), F32),
            pltpu.VMEM(adapter_up_weight.shape, BF),
            pltpu.SemaphoreType.DMA((2,)),
        ),
    )
    back = lax.all_to_all(back, "req", 0, 0)
    mine = lax.axis_index("tp").astype(I32).reshape(1)
    (base,) = call(
        base_kernel,
        (SM, VM, VM) + (VM,) * len(pairs) + (VM,),
        ((VM, shape((R * S, V), F32)),),
        (mine, x, far, *pairs, value_matrix),
        flops=10**8,
        mib=52,
    )
    step_values, attention = call(
        finish_kernel,
        (SM, VM, VM, VM, VM),
        ((VM, shape((R, S, V), BF)), (VM, shape((R, S, groups * HEAD_WIDTH), BF))),
        (place, back, base, attended, weights),
    )
    return (step_values, attention)


HALVES = 1


def solution(mesh):
    placed = (
        P("req", None, "tp"),
        P(None, "tp"),
        P("tp", "req"),
        P("req", "tp"),
        P("req"),
        P(),
        P("req"),
        P("req", None, "tp"),
        P("req", None, "tp"),
        P("req", None, "tp"),
        P("req", None, "tp"),
    )
    return jax.shard_map(
        body,
        mesh=mesh,
        in_specs=placed,
        out_specs=(P("req", None, "tp"), P("req", None, "tp")),
        check_vma=False,
    )
```

```python
import functools
import math

import jax
import jax.numpy as jnp
from jax import lax
from jax.experimental import pallas as pl
from jax.experimental.pallas import tpu as pltpu
from jax.sharding import PartitionSpec as P

HEAD_WIDTH = 128
ADAPTER_RANK = 64
QUERY_PER_KEY = 8
CAP = 2
LANES = 128
BF = jnp.bfloat16
F32 = jnp.float32
I32 = jnp.int32


def iota(shape, dim):
    return lax.broadcasted_iota(I32, shape, dim)


def dot(a, b):
    return jnp.dot(a, b, preferred_element_type=F32)


def picker(place, rows, steps, requests):
    shape = (rows, requests * steps)
    column = iota((1, requests * steps), 1)
    target = jnp.zeros((1, requests * steps), I32)
    for i in range(requests):
        target = jnp.where(column // steps == i, place[i] * steps + column % steps, target)
    return jnp.where(iota(shape, 0) == target, 1.0, 0.0).astype(BF)


def route_kernel(
    adapters, adapter_hbm, storage_hbm, x_hbm, send_ref, pick_ref, adapter_ref, storage_ref, x_ref, sems
):
    copies = [
        pltpu.make_async_copy(adapter_hbm, adapter_ref, sems.at[0]),
        pltpu.make_async_copy(storage_hbm, storage_ref, sems.at[1]),
        pltpu.make_async_copy(x_hbm, x_ref, sems.at[2]),
    ]
    for copy in copies:
        copy.start()
    requests, steps, width = x_ref.shape
    homes = send_ref.shape[0]
    rows = homes * CAP * steps
    copies[0].wait()
    copies[1].wait()
    storage = [storage_ref[adapter_ref[i]] for i in range(requests)]
    home = [s // adapters for s in storage]
    place = []
    code = jnp.zeros((requests * steps, LANES), I32)
    row = iota((requests * steps, LANES), 0)
    for i in range(requests):
        earlier = jnp.int32(0)
        for k in range(i):
            earlier = earlier + (home[k] == home[i]).astype(I32)
        place.append(home[i] * CAP + earlier)
        code = jnp.where(row // steps == i, storage[i] % adapters, code)
    pick = picker(place, rows, steps, requests)
    pick_ref[...] = pick
    copies[2].wait()
    x = x_ref[...].reshape(requests * steps, width)
    send = dot(pick, jnp.concatenate([x, code.astype(F32).astype(BF)], axis=1))
    send_ref[...] = send.astype(BF).reshape(send_ref.shape)


def down_kernel(halves, seen_ref, down_ref, part_ref, code_hbm, code_ref, sem):
    homes, per, width = seen_ref.shape
    width = width - LANES
    seen = seen_ref[...].reshape(homes * per, width + LANES)
    code = seen[:, width:].astype(F32)
    code_ref[...] = code
    save = pltpu.make_async_copy(code_ref, code_hbm, sem)
    save.start()
    product = dot(seen[:, :width], down_ref[...])
    lane = iota(code.shape, 1)
    own = jnp.zeros(code.shape, F32)
    for m in range(product.shape[1] // LANES):
        here = (2 * m + lane // ADAPTER_RANK).astype(F32) == code
        own = jnp.where(here, product[:, m * LANES : (m + 1) * LANES], own)
    own = own + pltpu.roll(own, ADAPTER_RANK, 1)
    half = own.shape[0] // 2
    part = jnp.where(iota((half, LANES), 1) < ADAPTER_RANK, own[:half], own[half:])
    pieces = []
    for _ in range(halves):
        high = part.astype(BF)
        pieces.append(high)
        part = part - high.astype(F32)
    part = jnp.concatenate(pieces, axis=0)
    for t in range(part_ref.shape[0]):
        part_ref[t] = part
    save.wait()


def up_kernel(halves, part_ref, code_hbm, up_ref, back_ref, code_ref, sem):
    load = pltpu.make_async_copy(code_hbm, code_ref, sem)
    load.start()
    half = code_ref.shape[0] // 2
    total = jnp.zeros((half, LANES), F32)
    for t in range(part_ref.shape[0]):
        for k in range(halves):
            total = total + part_ref[t, k * half : (k + 1) * half].astype(F32)
    total = total.astype(BF).astype(F32)
    turned = pltpu.roll(total, ADAPTER_RANK, 1)
    left = iota((half, LANES), 1) < ADAPTER_RANK
    both = jnp.concatenate(
        [jnp.where(left, total, turned), jnp.where(left, turned, total)], axis=0
    )
    load.wait()
    code = code_ref[...]
    lane = iota(code.shape, 1)
    spread = []
    for m in range(up_ref.shape[0] // LANES):
        here = (2 * m + lane // ADAPTER_RANK).astype(F32) == code
        spread.append(jnp.where(here, both, 0.0).astype(BF))
    back = dot(jnp.concatenate(spread, axis=1), up_ref[...]).astype(BF)
    back_ref[...] = back.reshape(back_ref.shape)


def scores_kernel(length_ref, q_ref, key_ref, value_ref, fresh_ref, part_ref, weight_ref):
    requests, steps, width = q_ref.shape
    context = key_ref.shape[1]
    groups = width // HEAD_WIDTH
    n = requests * steps
    scale = 1.0 / math.sqrt(HEAD_WIDTH)
    q = q_ref[...].reshape(n, width)
    q = jnp.concatenate(
        [q[:, g * HEAD_WIDTH : (g + 1) * HEAD_WIDTH] for g in range(groups)], axis=0
    )
    keys = key_ref[...].reshape(requests * context, HEAD_WIDTH)
    values = value_ref[...].reshape(requests * context, HEAD_WIDTH)
    fresh = fresh_ref[...].reshape(n, HEAD_WIDTH)
    contract = (((1,), (1,)), ((), ()))
    cached = lax.dot_general(q, keys, contract, preferred_element_type=F32) * scale
    new = lax.dot_general(q, fresh, contract, preferred_element_type=F32) * scale
    column = iota((1, requests * context), 1)
    limit = jnp.zeros((1, requests * context), I32)
    for i in range(requests):
        limit = jnp.where(column // context == i, length_ref[i], limit)
    owner = jnp.where(column % context < limit, column // context, -1)
    row = iota((groups * n, 1), 0) % n
    cached = jnp.where(row // steps == owner, cached, -jnp.inf)
    other = iota((1, n), 1)
    new = jnp.where(
        (row // steps == other // steps) & (other % steps <= row % steps), new, -jnp.inf
    )
    peak = jnp.maximum(
        jnp.max(cached, axis=1, keepdims=True), jnp.max(new, axis=1, keepdims=True)
    )
    cached = jnp.exp(cached - peak)
    new = jnp.exp(new - peak)
    total = jnp.sum(cached, axis=1, keepdims=True) + jnp.sum(new, axis=1, keepdims=True)
    weight_ref[...] = (new / total).astype(BF)
    part_ref[...] = dot((cached / total).astype(BF), values)


def partner(i, d):
    return ((((i + 1) & 7) ^ 1) + 7) & 7 if d == 3 else i ^ d


def base_kernel(index_ref, x_ref, far_ref, *refs):
    value_ref, base_ref = refs[-2:]
    requests, steps, width = x_ref.shape
    rows = requests * steps
    mine = index_ref[0]
    pieces = [(mine, x_ref[...]), (mine ^ 4, far_ref[...])]
    for k, ref in enumerate(refs[:-2]):
        other = partner(mine, k + 1)
        pieces.append((other, ref[:requests]))
        pieces.append((other ^ 4, ref[requests:]))
    total = jnp.zeros(base_ref.shape, F32)
    for other, piece in pieces:
        start = pl.multiple_of(other * width, width)
        total = total + dot(piece.reshape(rows, width), value_ref[pl.ds(start, width), :])
    base_ref[...] = total


def finish_kernel(pick_ref, back_ref, base_ref, part_ref, weight_ref, step_ref, out_ref):
    requests, steps, width = out_ref.shape
    homes, per, columns = back_ref.shape
    n = requests * steps
    back = back_ref[...].reshape(homes * per, columns)
    low = lax.dot_general(pick_ref[...], back, (((0,), (0,)), ((), ())), preferred_element_type=F32)
    step = (base_ref[...] + low).astype(BF)
    step_ref[...] = step.reshape(step_ref.shape)
    attended = (part_ref[...] + dot(weight_ref[...], step)).astype(BF)
    attended = jnp.concatenate(
        [attended[g * n : (g + 1) * n] for g in range(width // HEAD_WIDTH)], axis=1
    )
    out_ref[...] = attended.reshape(out_ref.shape)


VM = pl.BlockSpec(memory_space=pltpu.VMEM)
SM = pl.BlockSpec(memory_space=pltpu.SMEM)
HB = pl.BlockSpec(memory_space=pltpu.HBM)


def call(kernel, ins, outs, args, scratch=(), flops=0, bytes_accessed=0, mib=16):
    return pl.pallas_call(
        kernel,
        in_specs=list(ins),
        out_specs=tuple(s for s, _ in outs),
        out_shape=tuple(o for _, o in outs),
        scratch_shapes=list(scratch),
        compiler_params=pltpu.CompilerParams(vmem_limit_bytes=mib * 1024 * 1024),
        cost_estimate=pl.CostEstimate(
            flops=flops, bytes_accessed=bytes_accessed, transcendentals=0
        ),
    )(*args)


def body(
    normed_hidden_input,
    value_matrix,
    adapter_down_weight,
    adapter_up_weight,
    request_adapter,
    adapter_storage_row,
    cache_valid_length,
    queries,
    stored_key_cache,
    stored_value_cache,
    step_keys,
):
    x = normed_hidden_input
    R, S, W = x.shape
    V = value_matrix.shape[1]
    A = adapter_up_weight.shape[0] // ADAPTER_RANK
    H = lax.axis_size("req")
    T = lax.axis_size("tp")
    rows = H * CAP * S
    groups = queries.shape[2] // HEAD_WIDTH
    halves = HALVES
    shape = jax.ShapeDtypeStruct
    send, pick = call(
        functools.partial(route_kernel, A),
        (HB, HB, HB),
        ((VM, shape((H, CAP * S, W + LANES), BF)), (VM, shape((rows, R * S), BF))),
        (request_adapter, adapter_storage_row, x),
        (
            pltpu.SMEM(request_adapter.shape, I32),
            pltpu.SMEM(adapter_storage_row.shape, I32),
            pltpu.VMEM(x.shape, BF),
            pltpu.SemaphoreType.DMA((3,)),
        ),
        mib=60,
    )
    seen = lax.all_to_all(send, "req", 0, 0)
    x, send = lax.optimization_barrier((x, send))
    swap = lambda v, d: lax.ppermute(v, "tp", [(i, partner(i, d)) for i in range(T)])
    far = swap(x, 4)
    pair = jnp.concatenate([x, far], axis=0)
    pairs = [swap(pair, d) for d in (2, 1)]
    attended, weights = call(
        scores_kernel,
        (SM, VM, VM, VM, VM),
        ((VM, shape((groups * R * S, HEAD_WIDTH), F32)), (VM, shape((groups * R * S, R * S), BF))),
        (cache_valid_length, queries, stored_key_cache, stored_value_cache, step_keys),
        flops=10**8,
        bytes_accessed=10**6,
        mib=60,
    )
    seen, far, pair, pairs = lax.optimization_barrier((seen, far, pair, pairs))
    part, code = call(
        functools.partial(down_kernel, halves),
        (VM, VM),
        ((VM, shape((T, halves * rows // 2, LANES), BF)), (HB, shape((rows, LANES), F32))),
        (seen, adapter_down_weight),
        (pltpu.VMEM((rows, LANES), F32), pltpu.SemaphoreType.DMA),
    )
    part, pair = lax.optimization_barrier((part, pair))
    near = [swap(pair, d) for d in (3,)]
    part = lax.all_to_all(part, "tp", 0, 0)
    part, near, attended, weights = lax.optimization_barrier((part, near, attended, weights))
    pairs = [(pairs + near)[k] for k in (1, 0, 2)]
    (back,) = call(
        functools.partial(up_kernel, halves),
        (VM, HB, VM),
        ((VM, shape((H, CAP * S, V), BF)),),
        (part, code, adapter_up_weight),
        (pltpu.VMEM((rows, LANES), F32), pltpu.SemaphoreType.DMA),
    )
    back = lax.all_to_all(back, "req", 0, 0)
    mine = lax.axis_index("tp").astype(I32).reshape(1)
    (base,) = call(
        base_kernel,
        (SM, VM, VM) + (VM,) * len(pairs) + (VM,),
        ((VM, shape((R * S, V), F32)),),
        (mine, x, far, *pairs, value_matrix),
        flops=10**8,
        mib=52,
    )
    step_values, attention = call(
        finish_kernel,
        (VM, VM, VM, VM, VM),
        ((VM, shape((R, S, V), BF)), (VM, shape((R, S, groups * HEAD_WIDTH), BF))),
        (pick, back, base, attended, weights),
    )
    return (step_values, attention)


HALVES = 1


def solution(mesh):
    placed = (
        P("req", None, "tp"),
        P(None, "tp"),
        P("tp", "req"),
        P("req", "tp"),
        P("req"),
        P(),
        P("req"),
        P("req", None, "tp"),
        P("req", None, "tp"),
        P("req", None, "tp"),
        P("req", None, "tp"),
    )
    return jax.shard_map(
        body,
        mesh=mesh,
        in_specs=placed,
        out_specs=(P("req", None, "tp"), P("req", None, "tp")),
        check_vma=False,
    )
```

```python
import functools
import math

import jax
import jax.numpy as jnp
from jax import lax
from jax.experimental import pallas as pl
from jax.experimental.pallas import tpu as pltpu
from jax.sharding import PartitionSpec as P

HEAD_WIDTH = 128
ADAPTER_RANK = 64
QUERY_PER_KEY = 8
CAP = 2
LANES = 128
BF = jnp.bfloat16
F32 = jnp.float32
I32 = jnp.int32


def iota(shape, dim):
    return lax.broadcasted_iota(I32, shape, dim)


def dot(a, b):
    return jnp.dot(a, b, preferred_element_type=F32)


def picker(place, rows, steps, requests):
    shape = (rows, requests * steps)
    column = iota((1, requests * steps), 1)
    owner = lax.div(column, jnp.int32(steps))
    target = jnp.zeros((1, requests * steps), I32)
    for i in range(requests):
        target = jnp.where(owner == i, place[i] * steps, target)
    target = target + lax.rem(column, jnp.int32(steps))
    return jnp.where(iota(shape, 0) == target, 1.0, 0.0).astype(BF)


def route_kernel(
    adapters, adapter_hbm, storage_hbm, x_hbm, send_ref, pick_ref, adapter_ref, storage_ref, x_ref, sems
):
    copies = [
        pltpu.make_async_copy(adapter_hbm, adapter_ref, sems.at[0]),
        pltpu.make_async_copy(storage_hbm, storage_ref, sems.at[1]),
        pltpu.make_async_copy(x_hbm, x_ref, sems.at[2]),
    ]
    for copy in copies:
        copy.start()
    requests, steps, width = x_ref.shape
    homes = send_ref.shape[0]
    rows = homes * CAP * steps
    copies[0].wait()
    copies[1].wait()
    storage = [storage_ref[adapter_ref[i]] for i in range(requests)]
    home = [lax.div(s, jnp.int32(adapters)) for s in storage]
    place = []
    code = jnp.zeros((requests * steps, LANES), I32)
    owner = lax.div(iota((requests * steps, LANES), 0), jnp.int32(steps))
    for i in range(requests):
        earlier = jnp.int32(0)
        for k in range(i):
            earlier = earlier + (home[k] == home[i]).astype(I32)
        place.append(home[i] * CAP + earlier)
        code = jnp.where(owner == i, lax.rem(storage[i], jnp.int32(adapters)), code)
    pick = picker(place, rows, steps, requests)
    pick_ref[...] = pick
    copies[2].wait()
    x = x_ref[...].reshape(requests * steps, width)
    send = dot(pick, jnp.concatenate([x, code.astype(F32).astype(BF)], axis=1))
    send_ref[...] = send.astype(BF).reshape(send_ref.shape)


def down_kernel(halves, seen_ref, down_ref, part_hbm, code_hbm, part_ref, code_ref, sems):
    homes, per, width = seen_ref.shape
    width = width - LANES
    seen = seen_ref[...].reshape(homes * per, width + LANES)
    code_ref[...] = seen[:, width:]
    ranks = part_hbm.shape[0]
    saves = [pltpu.make_async_copy(code_ref, code_hbm, sems.at[ranks])]
    saves[0].start()
    code = seen[:, width:].astype(F32)
    product = dot(seen[:, :width], down_ref[...])
    lane = iota(code.shape, 1)
    own = jnp.zeros(code.shape, F32)
    for m in range(product.shape[1] // LANES):
        here = (2 * m + lane // ADAPTER_RANK).astype(F32) == code
        own = jnp.where(here, product[:, m * LANES : (m + 1) * LANES], own)
    own = own + pltpu.roll(own, ADAPTER_RANK, 1)
    half = own.shape[0] // 2
    part = jnp.where(iota((half, LANES), 1) < ADAPTER_RANK, own[:half], own[half:])
    pieces = []
    for _ in range(halves):
        high = part.astype(BF)
        pieces.append(high)
        part = part - high.astype(F32)
    part_ref[...] = jnp.concatenate(pieces, axis=0)
    for t in range(ranks):
        saves.append(pltpu.make_async_copy(part_ref, part_hbm.at[t], sems.at[t]))
        saves[-1].start()
    for save in saves:
        save.wait()


def up_kernel(halves, part_ref, code_hbm, up_ref, back_ref, code_ref, sem):
    load = pltpu.make_async_copy(code_hbm, code_ref, sem)
    load.start()
    half = code_ref.shape[0] // 2
    total = jnp.zeros((half, LANES), F32)
    for t in range(part_ref.shape[0]):
        for k in range(halves):
            total = total + part_ref[t, k * half : (k + 1) * half].astype(F32)
    total = total.astype(BF).astype(F32)
    turned = pltpu.roll(total, ADAPTER_RANK, 1)
    left = iota((half, LANES), 1) < ADAPTER_RANK
    both = jnp.concatenate(
        [jnp.where(left, total, turned), jnp.where(left, turned, total)], axis=0
    )
    load.wait()
    code = code_ref[...].astype(F32)
    lane = iota(code.shape, 1)
    spread = []
    for m in range(up_ref.shape[0] // LANES):
        here = (2 * m + lane // ADAPTER_RANK).astype(F32) == code
        spread.append(jnp.where(here, both, 0.0).astype(BF))
    back = dot(jnp.concatenate(spread, axis=1), up_ref[...]).astype(BF)
    back_ref[...] = back.reshape(back_ref.shape)


def scores_kernel(length_ref, q_ref, key_ref, value_ref, fresh_ref, part_ref, weight_ref):
    requests, steps, width = q_ref.shape
    context = key_ref.shape[1]
    groups = width // HEAD_WIDTH
    n = requests * steps
    scale = 1.0 / math.sqrt(HEAD_WIDTH)
    q = q_ref[...].reshape(n, width)
    q = jnp.concatenate(
        [q[:, g * HEAD_WIDTH : (g + 1) * HEAD_WIDTH] for g in range(groups)], axis=0
    )
    keys = key_ref[...].reshape(requests * context, HEAD_WIDTH)
    values = value_ref[...].reshape(requests * context, HEAD_WIDTH)
    fresh = fresh_ref[...].reshape(n, HEAD_WIDTH)
    contract = (((1,), (1,)), ((), ()))
    cached = lax.dot_general(q, keys, contract, preferred_element_type=F32) * scale
    new = lax.dot_general(q, fresh, contract, preferred_element_type=F32) * scale
    column = iota((1, requests * context), 1)
    limit = jnp.zeros((1, requests * context), I32)
    for i in range(requests):
        limit = jnp.where(column // context == i, length_ref[i], limit)
    owner = jnp.where(column % context < limit, column // context, -1)
    row = iota((groups * n, 1), 0) % n
    cached = jnp.where(row // steps == owner, cached, -jnp.inf)
    other = iota((1, n), 1)
    new = jnp.where(
        (row // steps == other // steps) & (other % steps <= row % steps), new, -jnp.inf
    )
    peak = jnp.maximum(
        jnp.max(cached, axis=1, keepdims=True), jnp.max(new, axis=1, keepdims=True)
    )
    cached = jnp.exp(cached - peak)
    new = jnp.exp(new - peak)
    total = jnp.sum(cached, axis=1, keepdims=True) + jnp.sum(new, axis=1, keepdims=True)
    weight_ref[...] = (new / total).astype(BF)
    part_ref[...] = dot((cached / total).astype(BF), values)


def partner(i, d):
    return ((((i + 1) & 7) ^ 1) + 7) & 7 if d == 3 else i ^ d


def base_kernel(index_ref, x_ref, far_ref, *refs):
    value_ref, base_ref = refs[-2:]
    requests, steps, width = x_ref.shape
    rows = requests * steps
    mine = index_ref[0]
    pieces = [(mine, x_ref[...]), (mine ^ 4, far_ref[...])]
    for k, ref in enumerate(refs[:-2]):
        other = partner(mine, k + 1)
        pieces.append((other, ref[:requests]))
        pieces.append((other ^ 4, ref[requests:]))
    total = jnp.zeros(base_ref.shape, F32)
    for other, piece in pieces:
        start = pl.multiple_of(other * width, width)
        total = total + dot(piece.reshape(rows, width), value_ref[pl.ds(start, width), :])
    base_ref[...] = total


def finish_kernel(pick_ref, back_ref, base_ref, part_ref, weight_ref, step_ref, out_ref):
    requests, steps, width = out_ref.shape
    homes, per, columns = back_ref.shape
    n = requests * steps
    back = back_ref[...].reshape(homes * per, columns)
    low = lax.dot_general(pick_ref[...], back, (((0,), (0,)), ((), ())), preferred_element_type=F32)
    step = (base_ref[...] + low).astype(BF)
    step_ref[...] = step.reshape(step_ref.shape)
    attended = (part_ref[...] + dot(weight_ref[...], step)).astype(BF)
    attended = jnp.concatenate(
        [attended[g * n : (g + 1) * n] for g in range(width // HEAD_WIDTH)], axis=1
    )
    out_ref[...] = attended.reshape(out_ref.shape)


VM = pl.BlockSpec(memory_space=pltpu.VMEM)
SM = pl.BlockSpec(memory_space=pltpu.SMEM)
HB = pl.BlockSpec(memory_space=pltpu.HBM)


def call(kernel, ins, outs, args, scratch=(), flops=0, bytes_accessed=0, mib=16):
    return pl.pallas_call(
        kernel,
        in_specs=list(ins),
        out_specs=tuple(s for s, _ in outs),
        out_shape=tuple(o for _, o in outs),
        scratch_shapes=list(scratch),
        compiler_params=pltpu.CompilerParams(vmem_limit_bytes=mib * 1024 * 1024),
        cost_estimate=pl.CostEstimate(
            flops=flops, bytes_accessed=bytes_accessed, transcendentals=0
        ),
    )(*args)


def body(
    normed_hidden_input,
    value_matrix,
    adapter_down_weight,
    adapter_up_weight,
    request_adapter,
    adapter_storage_row,
    cache_valid_length,
    queries,
    stored_key_cache,
    stored_value_cache,
    step_keys,
):
    x = normed_hidden_input
    R, S, W = x.shape
    V = value_matrix.shape[1]
    A = adapter_up_weight.shape[0] // ADAPTER_RANK
    H = lax.axis_size("req")
    T = lax.axis_size("tp")
    rows = H * CAP * S
    groups = queries.shape[2] // HEAD_WIDTH
    halves = HALVES
    shape = jax.ShapeDtypeStruct
    send, pick = call(
        functools.partial(route_kernel, A),
        (HB, HB, HB),
        ((VM, shape((H, CAP * S, W + LANES), BF)), (VM, shape((rows, R * S), BF))),
        (request_adapter, adapter_storage_row, x),
        (
            pltpu.SMEM(request_adapter.shape, I32),
            pltpu.SMEM(adapter_storage_row.shape, I32),
            pltpu.VMEM(x.shape, BF),
            pltpu.SemaphoreType.DMA((3,)),
        ),
        mib=60,
    )
    seen = lax.all_to_all(send, "req", 0, 0)
    x, send = lax.optimization_barrier((x, send))
    swap = lambda v, d: lax.ppermute(v, "tp", [(i, partner(i, d)) for i in range(T)])
    far = swap(x, 4)
    pair = jnp.concatenate([x, far], axis=0)
    pairs = [swap(pair, d) for d in (2, 1)]
    attended, weights = call(
        scores_kernel,
        (SM, VM, VM, VM, VM),
        ((VM, shape((groups * R * S, HEAD_WIDTH), F32)), (VM, shape((groups * R * S, R * S), BF))),
        (cache_valid_length, queries, stored_key_cache, stored_value_cache, step_keys),
        flops=10**8,
        bytes_accessed=10**6,
        mib=60,
    )
    seen, far, pair, pairs = lax.optimization_barrier((seen, far, pair, pairs))
    part, code = call(
        functools.partial(down_kernel, halves),
        (VM, VM),
        ((HB, shape((T, halves * rows // 2, LANES), BF)), (HB, shape((rows, LANES), BF))),
        (seen, adapter_down_weight),
        (
            pltpu.VMEM((halves * rows // 2, LANES), BF),
            pltpu.VMEM((rows, LANES), BF),
            pltpu.SemaphoreType.DMA((T + 1,)),
        ),
    )
    part, pair = lax.optimization_barrier((part, pair))
    near = [swap(pair, d) for d in (3,)]
    part = lax.all_to_all(part, "tp", 0, 0)
    part, near, attended, weights = lax.optimization_barrier((part, near, attended, weights))
    pairs = [(pairs + near)[k] for k in (1, 0, 2)]
    (back,) = call(
        functools.partial(up_kernel, halves),
        (VM, HB, VM),
        ((VM, shape((H, CAP * S, V), BF)),),
        (part, code, adapter_up_weight),
        (pltpu.VMEM((rows, LANES), BF), pltpu.SemaphoreType.DMA),
    )
    back = lax.all_to_all(back, "req", 0, 0)
    mine = lax.axis_index("tp").astype(I32).reshape(1)
    (base,) = call(
        base_kernel,
        (SM, VM, VM) + (VM,) * len(pairs) + (VM,),
        ((VM, shape((R * S, V), F32)),),
        (mine, x, far, *pairs, value_matrix),
        flops=10**8,
        mib=52,
    )
    step_values, attention = call(
        finish_kernel,
        (VM, VM, VM, VM, VM),
        ((VM, shape((R, S, V), BF)), (VM, shape((R, S, groups * HEAD_WIDTH), BF))),
        (pick, back, base, attended, weights),
    )
    return (step_values, attention)


HALVES = 1


def solution(mesh):
    placed = (
        P("req", None, "tp"),
        P(None, "tp"),
        P("tp", "req"),
        P("req", "tp"),
        P("req"),
        P(),
        P("req"),
        P("req", None, "tp"),
        P("req", None, "tp"),
        P("req", None, "tp"),
        P("req", None, "tp"),
    )
    return jax.shard_map(
        body,
        mesh=mesh,
        in_specs=placed,
        out_specs=(P("req", None, "tp"), P("req", None, "tp")),
        check_vma=False,
    )
```
